32 devices in a mesh: groups: 2 (over y), dom: 4 (over z), mem: 2 (over x), sub: 2 (over core).
Axes of the slice: x: 2, y: 2, z: 4, core: 2. Of those that a mesh axis runs over, the one named last changes fastest.
Arguments:
- ensemble: float32 [32, 65536], P('mem', ('groups', 'dom', 'sub')), parts along dimension 1
- station_cells: int32 [2048, 4], P('groups'), parts along dimension 0, may hold values from 0 to 4095, as said below
- owners: int32 [2048], P('groups'), parts along dimension 0, may hold values from 0 to 7
- interp_weights: float32 [2048, 4], P('groups'), parts along dimension 0
- station_order: int32 [2048], P('groups'), parts along dimension 0, may hold values from 0 to 1023, each once
- obs_values: float32 [2048], P('groups'), parts along dimension 0, may hold values from -6 to 6
- obs_var: float32 [2048], P('groups'), parts along dimension 0, may hold values from 0.2 to 2
- partners: int32 [1024, 16], P(('groups', 'dom', 'sub')), parts along dimension 0, may hold values from 0 to 511, as said below
Outputs:
- analysis: float32 [32, 65536], P('mem', ('groups', 'dom', 'sub')), parts along dimension 1
The draws below stay inside these ranges and needn't reach their ends.
There are 2 independent parts, one for each index of `groups`. The reference program is written for one: setup_inputs(seed, part) draws one part's arguments, and reference() takes and returns one part's arrays. A program takes and returns all parts, laid end to end along the dimension named above; each array names one. Nothing has to cross between parts.
Inputs may be any that keep to these rules, and one draw needn't show every extreme that they name: `station_cells`: the four cells of a station lie in one aligned block of 64 values. `partners`: each state block lists itself first; the other entries may repeat. `station_order`: a permutation of the stations.
All inputs are finite; a program needn't handle non-finite values.
Results may differ from the reference program's by a relative error of at most 0.0003.
Values sent between devices are 32-bit elements; how exact they have to be, the bound alone decides.
A program may use at most 64 MiB of HBM per device.

```python
import math
import jax
import jax.numpy as jnp
from jax import lax

S_DEV = 4096
BLOCK = 64
P_SIZE = 256
NBATCH = 4
PER = 16
M = 32
NPART = 8
S = 32768
NBLK = 512
NSTA = 1024


def draw_ensemble(key, part):
    key = jax.random.fold_in(key, 11)
    key_a, key_b, key_c, key_d, key_e = jax.random.split(key, 5)
    block_factor = jax.random.normal(key_a, (M, S // 64), jnp.float32)
    region_factor = jax.random.normal(key_b, (M, S // 1024), jnp.float32)
    cell_gain = jax.random.uniform(key_c, (S,), jnp.float32, 0.5, 1.5)
    mean_field = 0.5 * jax.random.normal(key_e, (S,), jnp.float32)
    cell_noise = jax.random.normal(key_d, (M, S), jnp.float32)
    shared = 0.8 * jnp.repeat(block_factor, 64, axis=1) + 0.6 * jnp.repeat(region_factor, 1024, axis=1)
    return mean_field[None, :] + cell_gain[None, :] * shared + 0.7 * cell_noise


def draw_station_cells(key, part):
    key = jax.random.fold_in(key, 12)
    key_a, key_b = jax.random.split(key)
    block_pick = jax.random.randint(key_a, (NSTA, 1), 0, S_DEV // 64)
    offsets = jax.random.randint(key_b, (NSTA, 4), 0, 64)
    spots = block_pick * 64 + offsets
    steps_four = jnp.arange(4, dtype=jnp.int32)
    spots = spots.at[0].set(S_DEV - 4 + steps_four)
    spots = spots.at[1].set(steps_four)
    return spots.astype(jnp.int32)


def draw_owners(key, part):
    key = jax.random.fold_in(key, 13)
    key_a, key_b = jax.random.split(key)
    first_pick = jax.random.randint(key_a, (NSTA,), 0, NPART)
    second_pick = jax.random.randint(key_b, (NSTA,), 0, NPART)
    chosen = jnp.minimum(first_pick, second_pick)
    chosen = chosen.at[0].set(NPART - 1)
    chosen = chosen.at[1].set(0)
    return chosen.astype(jnp.int32)


def draw_interp_weights(key, part):
    key = jax.random.fold_in(key, 14)
    raw_weights = jax.random.uniform(key, (NSTA, 4), jnp.float32, 0.2, 1.0)
    return raw_weights / jnp.sum(raw_weights, axis=1, keepdims=True)


def draw_partners(key, part):
    key = jax.random.fold_in(key, 15)
    key_a, key_b = jax.random.split(key)
    spatial = jax.random.permutation(key_a, NBLK).astype(jnp.int32)
    counting = jnp.arange(NBLK, dtype=jnp.int32)
    placed = jnp.zeros((NBLK,), jnp.int32).at[spatial].set(counting)
    offsets = jax.random.randint(key_b, (NBLK, PER - 1), -2 * PER, 2 * PER + 1).astype(jnp.int32)
    near_place = jnp.clip(placed[:, None] + offsets, 0, NBLK - 1)
    others = spatial[near_place]
    return jnp.concatenate([counting[:, None], others], axis=1).astype(jnp.int32)


def noise(rng, dims, scale, bound, kind=jnp.bfloat16):
    drawn = scale * jax.random.normal(rng, dims, jnp.float32)
    return jnp.clip(drawn, min=-bound, max=bound).astype(kind)


def setup_inputs(seed: int = 0, part: int = 0) -> dict:
    key_list = jax.random.split(jax.random.key(seed), 9)
    own_keys = jax.random.split(jax.random.fold_in(key_list[8], part), 9)
    ensemble = draw_ensemble(jax.random.fold_in(jax.random.fold_in(key_list[8], part), 71), part)
    station_cells = draw_station_cells(jax.random.fold_in(jax.random.fold_in(key_list[8], part), 71), part)
    owners = draw_owners(jax.random.fold_in(jax.random.fold_in(key_list[8], part), 71), part)
    interp_weights = draw_interp_weights(jax.random.fold_in(jax.random.fold_in(key_list[8], part), 71), part)
    station_order = jax.random.permutation(own_keys[4], NSTA).astype(jnp.int32)
    obs_values = noise(own_keys[5], (NSTA,), 1.5, 6.0, jnp.float32)
    obs_var = jnp.clip(jnp.exp(jax.random.uniform(own_keys[6], (NSTA,), jnp.float32, math.log(0.2), math.log(2.0))), 0.2, 2.0)
    partners = draw_partners(jax.random.fold_in(jax.random.fold_in(key_list[8], part), 71), part)
    return dict(ensemble=ensemble, station_cells=station_cells, owners=owners, interp_weights=interp_weights, station_order=station_order, obs_values=obs_values, obs_var=obs_var, partners=partners)


def increments(obs_prior, observed, noise_var):
    member_count = obs_prior.shape[0]
    mean_prior = lax.optimization_barrier(jnp.mean(obs_prior, axis=0))
    spread = obs_prior - mean_prior[None, :]
    variance = lax.optimization_barrier(jnp.sum(spread * spread, axis=0)) / (member_count - 1)
    shrink_ratio = jnp.sqrt(noise_var / (variance + noise_var))
    posterior = (noise_var * mean_prior + variance * observed) / (variance + noise_var)
    obs_shift = (posterior - mean_prior)[None, :] + (shrink_ratio - 1.0)[None, :] * spread
    gain_factor = 1.0 / ((variance + 1e-05) * (member_count - 1))
    return (spread, obs_shift, gain_factor)

def reference(ensemble, station_cells, owners, interp_weights, station_order, obs_values, obs_var, partners):
    member_count = ensemble.shape[0]
    total_cells = ensemble.shape[1]
    blocks_dev = S_DEV // BLOCK
    part_states = ensemble.reshape(member_count, NPART, S_DEV).transpose(1, 0, 2)
    link_rows = partners.reshape(NPART, blocks_dev, PER)
    for batch_index in range(NBATCH):
        picked = station_order[batch_index * P_SIZE:(batch_index + 1) * P_SIZE]
        owner_part = owners[picked]
        spot_cells = station_cells[picked]
        interp = interp_weights[picked]
        global_cell = (owner_part[:, None] * S_DEV + spot_cells).astype(jnp.int32)
        flat_state = part_states.transpose(1, 0, 2).reshape(member_count, total_cells)
        obs_prior = lax.optimization_barrier(jnp.sum(flat_state[:, global_cell] * interp[None], axis=2))
        spread, obs_shift, gain_factor = increments(obs_prior, obs_values[picked], obs_var[picked])
        stat_block = (owner_part * blocks_dev + spot_cells[:, 0] // BLOCK).astype(jnp.int32)

        def adjust(operands):
            block_state, block_links = operands
            nearby = jnp.any(block_links[:, :, None] == stat_block[None, None, :], axis=1).astype(jnp.float32)
            gain_scale = nearby * gain_factor[None, :]
            cross_cov = jnp.einsum('mc,mp->cp', block_state, spread, precision=lax.Precision.HIGHEST)
            gain_matrix = (cross_cov.reshape(blocks_dev, BLOCK, P_SIZE) * gain_scale[:, None, :]).reshape(S_DEV, P_SIZE)
            return block_state + jnp.einsum('mp,cp->mc', obs_shift, gain_matrix, precision=lax.Precision.HIGHEST)
        part_states = lax.map(adjust, (part_states, link_rows))
    return part_states.transpose(1, 0, 2).reshape(member_count, total_cells)
```

```python
import functools

import jax
import jax.numpy as jnp
from jax import lax
from jax.experimental import pallas as pl
from jax.experimental.pallas import tpu as pltpu
from jax.sharding import PartitionSpec as P

BLOCK = 64
P_SIZE = 256
NBATCH = 4
LANES = 128
CHUNK = 2048
F32 = jnp.float32
BF16 = jnp.bfloat16


def pieces(value, count):
    found = []
    for _ in range(count):
        head = value.astype(BF16).astype(F32)
        found.append(head)
        value = value - head
    return found


def halves(value):
    head = value.astype(BF16)
    return head, (value - head.astype(F32)).astype(BF16)


def dot(left, right):
    return lax.dot_general(left, right, (((1,), (0,)), ((), ())), preferred_element_type=F32)


def dot_first(left, right):
    return lax.dot_general(left, right, (((0,), (0,)), ((), ())), preferred_element_type=F32)


def kernel(
    sizes,
    x_ref, links_ref, cells_ref, owners_ref, interp_ref, order_ref, obs_ref, noise_ref,
    out_ref,
    everyone, link_slots, contrib, parts_in, priors, perm, links_t, hot_t, near_t,
    mask_st, mask_cells, stations, gains, shifts,
    x_send, x_recv, l_send, l_recv, r_send, r_recv, g_send, g_recv,
):
    nparts, nsub, nmem, nred = sizes
    rows, width = x_ref.shape
    blocks = width // BLOCK
    nblk = nparts * blocks
    members = rows * nmem
    nsta = order_ref.shape[1]
    piece = nsta // nred
    total = nparts * nmem
    part = lax.axis_index("dom") * nsub + lax.axis_index("sub")
    mem = lax.axis_index("mem")
    me = part * nmem + mem

    def place(which, member):
        return {"dom": which // nsub, "mem": member, "sub": which % nsub}

    def each(count, act):
        if count <= 16:
            for k in range(1, count):
                act(k)
        else:
            lax.fori_loop(1, count, lambda k, c: (act(k), c)[1], 0)

    def only(condition, act):
        if nred == nparts:
            act()
        else:
            pl.when(condition)(act)

    barrier = pltpu.get_barrier_semaphore()

    def greet(k):
        to = lax.rem(me + k, total)
        pl.semaphore_signal(
            barrier, inc=1, device_id=place(to // nmem, to % nmem),
            device_id_type=pl.DeviceIdType.MESH,
        )

    each(total, greet)
    pl.semaphore_wait(barrier, total - 1)

    my_rows = pl.ds(pl.multiple_of(mem * rows, rows), rows)

    def copy_x(k):
        return pltpu.make_async_remote_copy(
            src_ref=x_ref, dst_ref=everyone.at[my_rows, :],
            send_sem=x_send.at[k - 1], recv_sem=x_recv.at[k - 1],
            device_id=place(part, lax.rem(mem + k, nmem)),
            device_id_type=pl.DeviceIdType.MESH,
        )

    def copy_links(k):
        return pltpu.make_async_remote_copy(
            src_ref=links_ref, dst_ref=link_slots.at[part],
            send_sem=l_send.at[k - 1], recv_sem=l_recv.at[k - 1],
            device_id=place(lax.rem(part + k, nparts), mem),
            device_id_type=pl.DeviceIdType.MESH,
        )

    def copy_part(k):
        to = lax.rem(part + k, nparts)
        return pltpu.make_async_remote_copy(
            src_ref=contrib.at[lax.rem(to, nred)], dst_ref=parts_in.at[part],
            send_sem=r_send.at[k - 1], recv_sem=r_recv.at[k - 1],
            device_id=place(to, mem), device_id_type=pl.DeviceIdType.MESH,
        )

    def my_prior():
        column = pl.multiple_of(lax.rem(part, nred) * piece, piece)
        return priors.at[my_rows, pl.ds(column, piece)]

    def copy_prior(k):
        to = lax.rem(me + k, total)
        return pltpu.make_async_remote_copy(
            src_ref=my_prior(), dst_ref=my_prior(),
            send_sem=g_send.at[k - 1], recv_sem=g_recv.at[k - 1],
            device_id=place(to // nmem, to % nmem), device_id_type=pl.DeviceIdType.MESH,
        )

    each(nparts, lambda k: copy_links(k).start())
    each(nmem, lambda k: copy_x(k).start())

    cells = cells_ref[...]
    within = cells % LANES
    lane_of = lax.broadcasted_iota(jnp.int32, (LANES, nsta), 0)
    weights = jnp.zeros((LANES, nsta), F32)
    for k in range(cells.shape[0]):
        weights += jnp.where(lane_of == within[k : k + 1, :], interp_ref[k : k + 1, :], 0.0)
    w_hi, w_lo = halves(weights)
    tiles = width // LANES
    x_rows = jnp.concatenate(
        [x_ref[:, t * LANES : (t + 1) * LANES] for t in range(tiles)], axis=0
    )
    x_hi, x_lo = halves(x_rows)
    seen = dot(
        jnp.concatenate([x_hi, x_hi, x_lo], axis=1), jnp.concatenate([w_hi, w_lo, w_hi], axis=0)
    )
    owners = owners_ref[...]
    tile_of = (owners - part) * tiles + cells[0:1, :] // LANES
    share = jnp.zeros((rows, nsta), F32)
    for t in range(tiles):
        share += jnp.where(tile_of == t, seen[t * rows : (t + 1) * rows, :], 0.0)
    for r in range(nred):
        contrib[r] = share[:, r * piece : (r + 1) * piece]
    each(
        nparts,
        lambda k: only(lax.rem(part + k, nparts) < nred, lambda: copy_part(k).start()),
    )
    parts_in[part] = contrib[lax.rem(part, nred)]
    link_slots[part] = links_ref[...]
    everyone[my_rows, :] = x_ref[...]

    order = order_ref[...]
    strip = P_SIZE

    def build_perm(t, carry):
        first = pl.multiple_of(t * strip, strip)
        station = lax.broadcasted_iota(jnp.int32, (strip, nsta), 0) + first
        perm[pl.ds(first, strip), :] = (station == order).astype(F32).astype(BF16)
        return carry

    lax.fori_loop(0, nsta // strip, build_perm, 0)
    listed = jnp.concatenate(
        [owners.astype(F32), (cells[0:1, :] // BLOCK).astype(F32)]
        + pieces(obs_ref[...], 3)
        + pieces(noise_ref[...], 3),
        axis=0,
    )
    listed = dot(listed.astype(BF16), perm[...])
    station_block = (listed[0:1, :] * blocks + listed[1:2, :]).astype(jnp.int32)
    observed = listed[2:3, :] + listed[3:4, :] + listed[4:5, :]
    noise_var = listed[5:6, :] + listed[6:7, :] + listed[7:8, :]

    def reduce_shares():
        each(nparts, lambda k: copy_part(k).wait_recv())
        summed = parts_in[0]
        for q in range(1, nparts):
            summed += parts_in[q]
        my_prior()[...] = summed
        each(total, lambda k: copy_prior(k).start())

    only(part < nred, reduce_shares)
    each(
        nparts,
        lambda k: only(lax.rem(part + k, nparts) < nred, lambda: copy_part(k).wait_send()),
    )

    each(nparts, lambda k: copy_links(k).wait())
    all_links = jnp.concatenate([link_slots[q] for q in range(nparts)], axis=1)

    def build_links(t, carry):
        first = pl.multiple_of(t * BLOCK, BLOCK)
        block = lax.broadcasted_iota(jnp.int32, (BLOCK, nblk), 0) + first
        hit = block == all_links[0:1, :]
        for k in range(1, all_links.shape[0]):
            hit = hit | (block == all_links[k : k + 1, :])
        links_t[pl.ds(first, BLOCK), :] = hit.astype(F32).astype(BF16)
        block = lax.broadcasted_iota(jnp.int32, (BLOCK, nsta), 0) + first
        hot_t[pl.ds(first, BLOCK), :] = (block == station_block).astype(F32).astype(BF16)
        return carry

    lax.fori_loop(0, nparts, build_links, 0)
    local_block = lax.broadcasted_iota(jnp.int32, (blocks, width), 0)
    local_cell = lax.broadcasted_iota(jnp.int32, (blocks, width), 1)
    spread_out = (local_cell // BLOCK == local_block).astype(F32).astype(BF16)
    block_col = lax.broadcasted_iota(jnp.int32, (nblk, blocks), 0)
    block_row = lax.broadcasted_iota(jnp.int32, (nblk, blocks), 1)
    mine = (block_col == block_row + part * blocks).astype(F32).astype(BF16)
    for b in range(NBATCH):
        span = slice(b * P_SIZE, (b + 1) * P_SIZE)
        near = dot_first(hot_t[:, span], links_t[...]).astype(BF16)
        if b + 1 < NBATCH:
            mask_st[span, (b + 1) * P_SIZE :] = dot(near, hot_t[:, (b + 1) * P_SIZE :]).astype(BF16)
        near_t[span, :] = dot(near, mine).astype(BF16)

    def build_mask(t, carry):
        first = pl.multiple_of(t * P_SIZE, P_SIZE)
        near = near_t[pl.ds(first, P_SIZE), :]
        mask_cells[pl.ds(first, P_SIZE), :] = dot(near, spread_out).astype(BF16)
        return carry

    lax.fori_loop(0, NBATCH, build_mask, 0)

    def prior_sent(k):
        only(part < nred, lambda: copy_prior(k).wait_send())
        sender = lax.rem(me + total - k, total)
        only(sender // nmem < nred, lambda: copy_prior(k).wait_recv())

    each(total, prior_sent)
    ordered = dot(jnp.concatenate(pieces(priors[...], 3), axis=0).astype(BF16), perm[...])
    stations[...] = (
        ordered[:members] + ordered[members : 2 * members] + ordered[2 * members :]
    )

    def step(b, state, mask):
        high, low = halves(state)
        cross = dot(gains[b], jnp.concatenate([high, high, low], axis=0))
        c_hi, c_lo = halves(cross)
        shift = shifts[b]
        z_hi = c_hi * mask
        return state + dot(
            jnp.concatenate([shift[:members], shift[members:], shift[:members]], axis=1),
            jnp.concatenate([z_hi, z_hi, c_lo * mask], axis=0),
        )

    for b in range(NBATCH):
        span = slice(b * P_SIZE, (b + 1) * P_SIZE)
        prior = stations[:, span]
        noise_b, observed_b = noise_var[:, span], observed[:, span]
        mean = jnp.sum(prior, axis=0, keepdims=True) / members
        spread = prior - mean
        variance = jnp.sum(spread * spread, axis=0, keepdims=True) / (members - 1)
        ratio = jnp.sqrt(noise_b / (variance + noise_b))
        posterior = (noise_b * mean + variance * observed_b) / (variance + noise_b)
        shift = posterior - mean + (ratio - 1.0) * spread
        gain = spread / ((variance + 1e-05) * (members - 1))
        g_hi, g_lo = pieces(gain, 2)
        gains[b] = jnp.concatenate([g_hi, g_lo, g_hi], axis=0).T.astype(BF16)
        shifts[b] = jnp.concatenate(pieces(shift, 2), axis=0).astype(BF16)
        if b + 1 < NBATCH:
            later = slice((b + 1) * P_SIZE, nsta)
            stations[:, later] = step(b, stations[:, later], mask_st[span, later])

    each(nmem, lambda k: copy_x(k).wait())
    chunk = min(CHUNK, width)

    for b in range(NBATCH):

        def update(t, carry):
            columns = pl.ds(pl.multiple_of(t * chunk, chunk), chunk)
            mask = mask_cells[b * P_SIZE : (b + 1) * P_SIZE, columns]
            everyone[:, columns] = step(b, everyone[:, columns], mask)
            return carry

        lax.fori_loop(0, width // chunk, update, 0)
    out_ref[...] = everyone[my_rows, :]


def body(
    sizes, ensemble, station_cells, owners, interp_weights, station_order, obs_values, obs_var,
    partners,
):
    nparts, nsub, nmem, nred = sizes
    rows, width = ensemble.shape
    blocks, listed = partners.shape
    nsta = owners.shape[0]
    members, nblk, total = rows * nmem, nparts * blocks, nparts * nmem
    piece = nsta // nred
    dma = pltpu.SemaphoreType.DMA
    return pl.pallas_call(
        functools.partial(kernel, sizes),
        out_shape=jax.ShapeDtypeStruct((rows, width), F32),
        in_specs=[pl.BlockSpec(memory_space=pltpu.VMEM)] * 8,
        out_specs=pl.BlockSpec(memory_space=pltpu.VMEM),
        scratch_shapes=[
            pltpu.VMEM((members, width), F32),
            pltpu.VMEM((nparts, listed, blocks), jnp.int32),
            pltpu.VMEM((nred, rows, piece), F32),
            pltpu.VMEM((nparts, rows, piece), F32),
            pltpu.VMEM((members, nsta), F32),
            pltpu.VMEM((nsta, nsta), BF16),
            pltpu.VMEM((nblk, nblk), BF16),
            pltpu.VMEM((nblk, nsta), BF16),
            pltpu.VMEM((nsta, blocks), BF16),
            pltpu.VMEM((nsta, nsta), BF16),
            pltpu.VMEM((nsta, width), BF16),
            pltpu.VMEM((members, nsta), F32),
            pltpu.VMEM((NBATCH, P_SIZE, 3 * members), BF16),
            pltpu.VMEM((NBATCH, 2 * members, P_SIZE), BF16),
            dma((max(nmem - 1, 1),)),
            dma((max(nmem - 1, 1),)),
            dma((max(nparts - 1, 1),)),
            dma((max(nparts - 1, 1),)),
            dma((max(nparts - 1, 1),)),
            dma((max(nparts - 1, 1),)),
            dma((max(total - 1, 1),)),
            dma((max(total - 1, 1),)),
        ],
        compiler_params=pltpu.CompilerParams(
            collective_id=0, has_side_effects=True, vmem_limit_bytes=56 * 1024 * 1024
        ),
    )(
        ensemble, partners.T, station_cells.T, owners[None], interp_weights.T,
        station_order[None], obs_values[None], obs_var[None],
    )


def solution(mesh):
    nsub, nmem = mesh.shape["sub"], mesh.shape["mem"]
    nparts = mesh.shape["dom"] * nsub

    def local(*arrays):
        nred = min(nparts, arrays[2].shape[0] // LANES)
        return body((nparts, nsub, nmem, nred), *arrays)

    return jax.shard_map(
        local,
        mesh=mesh,
        in_specs=(
            P("mem", ("groups", "dom", "sub")),
            P("groups", None),
            P("groups"),
            P("groups", None),
            P("groups"),
            P("groups"),
            P("groups"),
            P(("groups", "dom", "sub"), None),
        ),
        out_specs=P("mem", ("groups", "dom", "sub")),
        check_vma=False,
    )
```

```python
import functools

import jax
import jax.numpy as jnp
from jax import lax
from jax.experimental import pallas as pl
from jax.experimental.pallas import tpu as pltpu
from jax.sharding import PartitionSpec as P

BLOCK = 64
P_SIZE = 256
NBATCH = 4
LANES = 128
CHUNK = 2048
F32 = jnp.float32
BF16 = jnp.bfloat16


def pieces(value, count):
    found = []
    for _ in range(count):
        head = value.astype(BF16).astype(F32)
        found.append(head)
        value = value - head
    return found


def halves(value):
    head = value.astype(BF16)
    return head, (value - head.astype(F32)).astype(BF16)


def dot(left, right):
    return lax.dot_general(left, right, (((1,), (0,)), ((), ())), preferred_element_type=F32)


def dot_first(left, right):
    return lax.dot_general(left, right, (((0,), (0,)), ((), ())), preferred_element_type=F32)


def kernel(
    sizes,
    x_ref, links_ref, cells_ref, owners_ref, interp_ref, order_ref, obs_ref, noise_ref,
    out_ref,
    everyone, link_slots, contrib, parts_in, priors, perm, links_t, hot_t, near_t,
    mask_st, mask_cells, stations, gains, shifts,
    x_send, x_recv, l_send, l_recv, r_send, r_recv, g_send, g_recv,
):
    nparts, nsub, nmem, nred = sizes
    rows, width = x_ref.shape
    blocks = width // BLOCK
    nblk = nparts * blocks
    members = rows * nmem
    nsta = order_ref.shape[1]
    piece = nsta // nred
    total = nparts * nmem
    part = lax.axis_index("dom") * nsub + lax.axis_index("sub")
    mem = lax.axis_index("mem")
    me = part * nmem + mem

    def place(which, member):
        return {"dom": which // nsub, "mem": member, "sub": which % nsub}

    def each(count, act):
        if count <= 16:
            for k in range(1, count):
                act(k)
        else:
            lax.fori_loop(1, count, lambda k, c: (act(k), c)[1], 0)

    def only(condition, act):
        if nred == nparts:
            act()
        else:
            pl.when(condition)(act)

    barrier = pltpu.get_barrier_semaphore()

    def greet(k):
        to = lax.rem(me + k, total)
        pl.semaphore_signal(
            barrier, inc=1, device_id=place(to // nmem, to % nmem),
            device_id_type=pl.DeviceIdType.MESH,
        )

    each(total, greet)
    my_rows = pl.ds(pl.multiple_of(mem * rows, rows), rows)

    def copy_x(k):
        return pltpu.make_async_remote_copy(
            src_ref=x_ref, dst_ref=everyone.at[my_rows, :],
            send_sem=x_send.at[k - 1], recv_sem=x_recv.at[k - 1],
            device_id=place(part, lax.rem(mem + k, nmem)),
            device_id_type=pl.DeviceIdType.MESH,
        )

    def copy_links(k):
        return pltpu.make_async_remote_copy(
            src_ref=links_ref, dst_ref=link_slots.at[part],
            send_sem=l_send.at[k - 1], recv_sem=l_recv.at[k - 1],
            device_id=place(lax.rem(part + k, nparts), mem),
            device_id_type=pl.DeviceIdType.MESH,
        )

    def copy_part(k):
        to = lax.rem(part + k, nparts)
        return pltpu.make_async_remote_copy(
            src_ref=contrib.at[lax.rem(to, nred)], dst_ref=parts_in.at[part],
            send_sem=r_send.at[k - 1], recv_sem=r_recv.at[k - 1],
            device_id=place(to, mem), device_id_type=pl.DeviceIdType.MESH,
        )

    def my_prior():
        column = pl.multiple_of(lax.rem(part, nred) * piece, piece)
        return priors.at[my_rows, pl.ds(column, piece)]

    def copy_prior(k):
        to = lax.rem(me + k, total)
        return pltpu.make_async_remote_copy(
            src_ref=my_prior(), dst_ref=my_prior(),
            send_sem=g_send.at[k - 1], recv_sem=g_recv.at[k - 1],
            device_id=place(to // nmem, to % nmem), device_id_type=pl.DeviceIdType.MESH,
        )

    cells = cells_ref[...]
    within = cells % LANES
    lane_of = lax.broadcasted_iota(jnp.int32, (LANES, nsta), 0)
    weights = jnp.zeros((LANES, nsta), F32)
    for k in range(cells.shape[0]):
        weights += jnp.where(lane_of == within[k : k + 1, :], interp_ref[k : k + 1, :], 0.0)
    w_hi, w_lo = halves(weights)
    tiles = width // LANES
    x_rows = jnp.concatenate(
        [x_ref[:, t * LANES : (t + 1) * LANES] for t in range(tiles)], axis=0
    )
    x_hi, x_lo = halves(x_rows)
    seen = dot(
        jnp.concatenate([x_hi, x_hi, x_lo], axis=1), jnp.concatenate([w_hi, w_lo, w_hi], axis=0)
    )
    owners = owners_ref[...]
    tile_of = (owners - part) * tiles + cells[0:1, :] // LANES
    share = jnp.zeros((rows, nsta), F32)
    for t in range(tiles):
        share += jnp.where(tile_of == t, seen[t * rows : (t + 1) * rows, :], 0.0)
    for r in range(nred):
        contrib[r] = share[:, r * piece : (r + 1) * piece]
    pl.semaphore_wait(barrier, total - 1)
    each(
        nparts,
        lambda k: only(lax.rem(part + k, nparts) < nred, lambda: copy_part(k).start()),
    )
    each(nparts, lambda k: copy_links(k).start())
    each(nmem, lambda k: copy_x(k).start())
    parts_in[part] = contrib[lax.rem(part, nred)]
    link_slots[part] = links_ref[...]
    everyone[my_rows, :] = x_ref[...]

    order = order_ref[...]
    strip = P_SIZE

    def build_perm(t, carry):
        first = pl.multiple_of(t * strip, strip)
        station = lax.broadcasted_iota(jnp.int32, (strip, nsta), 0) + first
        perm[pl.ds(first, strip), :] = (station == order).astype(F32).astype(BF16)
        return carry

    lax.fori_loop(0, nsta // strip, build_perm, 0)
    listed = jnp.concatenate(
        [owners.astype(F32), (cells[0:1, :] // BLOCK).astype(F32)]
        + pieces(obs_ref[...], 3)
        + pieces(noise_ref[...], 3),
        axis=0,
    )
    listed = dot(listed.astype(BF16), perm[...])
    station_block = (listed[0:1, :] * blocks + listed[1:2, :]).astype(jnp.int32)
    observed = listed[2:3, :] + listed[3:4, :] + listed[4:5, :]
    noise_var = listed[5:6, :] + listed[6:7, :] + listed[7:8, :]

    def reduce_shares():
        each(nparts, lambda k: copy_part(k).wait_recv())
        summed = parts_in[0]
        for q in range(1, nparts):
            summed += parts_in[q]
        my_prior()[...] = summed
        each(total, lambda k: copy_prior(k).start())

    only(part < nred, reduce_shares)
    each(
        nparts,
        lambda k: only(lax.rem(part + k, nparts) < nred, lambda: copy_part(k).wait_send()),
    )

    each(nparts, lambda k: copy_links(k).wait())
    all_links = jnp.concatenate([link_slots[q] for q in range(nparts)], axis=1)

    def build_links(t, carry):
        first = pl.multiple_of(t * BLOCK, BLOCK)
        block = lax.broadcasted_iota(jnp.int32, (BLOCK, nblk), 0) + first
        hit = block == all_links[0:1, :]
        for k in range(1, all_links.shape[0]):
            hit = hit | (block == all_links[k : k + 1, :])
        links_t[pl.ds(first, BLOCK), :] = hit.astype(F32).astype(BF16)
        block = lax.broadcasted_iota(jnp.int32, (BLOCK, nsta), 0) + first
        hot_t[pl.ds(first, BLOCK), :] = (block == station_block).astype(F32).astype(BF16)
        return carry

    lax.fori_loop(0, nparts, build_links, 0)
    local_block = lax.broadcasted_iota(jnp.int32, (blocks, width), 0)
    local_cell = lax.broadcasted_iota(jnp.int32, (blocks, width), 1)
    spread_out = (local_cell // BLOCK == local_block).astype(F32).astype(BF16)
    block_col = lax.broadcasted_iota(jnp.int32, (nblk, blocks), 0)
    block_row = lax.broadcasted_iota(jnp.int32, (nblk, blocks), 1)
    mine = (block_col == block_row + part * blocks).astype(F32).astype(BF16)
    for b in range(NBATCH):
        span = slice(b * P_SIZE, (b + 1) * P_SIZE)
        near = dot_first(hot_t[:, span], links_t[...]).astype(BF16)
        if b + 1 < NBATCH:
            mask_st[span, (b + 1) * P_SIZE :] = dot(near, hot_t[:, (b + 1) * P_SIZE :]).astype(BF16)
        near_t[span, :] = dot(near, mine).astype(BF16)

    def build_mask(t, carry):
        first = pl.multiple_of(t * P_SIZE, P_SIZE)
        near = near_t[pl.ds(first, P_SIZE), :]
        mask_cells[pl.ds(first, P_SIZE), :] = dot(near, spread_out).astype(BF16)
        return carry

    lax.fori_loop(0, NBATCH, build_mask, 0)

    def prior_sent(k):
        only(part < nred, lambda: copy_prior(k).wait_send())
        sender = lax.rem(me + total - k, total)
        only(sender // nmem < nred, lambda: copy_prior(k).wait_recv())

    each(total, prior_sent)
    ordered = dot(jnp.concatenate(pieces(priors[...], 3), axis=0).astype(BF16), perm[...])
    stations[...] = (
        ordered[:members] + ordered[members : 2 * members] + ordered[2 * members :]
    )

    def step(b, state, mask):
        high, low = halves(state)
        cross = dot(gains[b], jnp.concatenate([high, high, low], axis=0))
        c_hi, c_lo = halves(cross)
        shift = shifts[b]
        z_hi = c_hi * mask
        return state + dot(
            jnp.concatenate([shift[:members], shift[members:], shift[:members]], axis=1),
            jnp.concatenate([z_hi, z_hi, c_lo * mask], axis=0),
        )

    for b in range(NBATCH):
        span = slice(b * P_SIZE, (b + 1) * P_SIZE)
        prior = stations[:, span]
        noise_b, observed_b = noise_var[:, span], observed[:, span]
        mean = jnp.sum(prior, axis=0, keepdims=True) / members
        spread = prior - mean
        variance = jnp.sum(spread * spread, axis=0, keepdims=True) / (members - 1)
        ratio = jnp.sqrt(noise_b / (variance + noise_b))
        posterior = (noise_b * mean + variance * observed_b) / (variance + noise_b)
        shift = posterior - mean + (ratio - 1.0) * spread
        gain = spread / ((variance + 1e-05) * (members - 1))
        g_hi, g_lo = pieces(gain, 2)
        gains[b] = jnp.concatenate([g_hi, g_lo, g_hi], axis=0).T.astype(BF16)
        shifts[b] = jnp.concatenate(pieces(shift, 2), axis=0).astype(BF16)
        if b + 1 < NBATCH:
            later = slice((b + 1) * P_SIZE, nsta)
            stations[:, later] = step(b, stations[:, later], mask_st[span, later])

    each(nmem, lambda k: copy_x(k).wait())
    chunk = min(CHUNK, width)

    for b in range(NBATCH):

        def update(t, carry):
            columns = pl.ds(pl.multiple_of(t * chunk, chunk), chunk)
            mask = mask_cells[b * P_SIZE : (b + 1) * P_SIZE, columns]
            everyone[:, columns] = step(b, everyone[:, columns], mask)
            return carry

        lax.fori_loop(0, width // chunk, update, 0)
    out_ref[...] = everyone[my_rows, :]


def body(
    sizes, ensemble, station_cells, owners, interp_weights, station_order, obs_values, obs_var,
    partners,
):
    nparts, nsub, nmem, nred = sizes
    rows, width = ensemble.shape
    blocks, listed = partners.shape
    nsta = owners.shape[0]
    members, nblk, total = rows * nmem, nparts * blocks, nparts * nmem
    piece = nsta // nred
    dma = pltpu.SemaphoreType.DMA
    return pl.pallas_call(
        functools.partial(kernel, sizes),
        out_shape=jax.ShapeDtypeStruct((rows, width), F32),
        in_specs=[pl.BlockSpec(memory_space=pltpu.VMEM)] * 8,
        out_specs=pl.BlockSpec(memory_space=pltpu.VMEM),
        scratch_shapes=[
            pltpu.VMEM((members, width), F32),
            pltpu.VMEM((nparts, listed, blocks), jnp.int32),
            pltpu.VMEM((nred, rows, piece), F32),
            pltpu.VMEM((nparts, rows, piece), F32),
            pltpu.VMEM((members, nsta), F32),
            pltpu.VMEM((nsta, nsta), BF16),
            pltpu.VMEM((nblk, nblk), BF16),
            pltpu.VMEM((nblk, nsta), BF16),
            pltpu.VMEM((nsta, blocks), BF16),
            pltpu.VMEM((nsta, nsta), BF16),
            pltpu.VMEM((nsta, width), BF16),
            pltpu.VMEM((members, nsta), F32),
            pltpu.VMEM((NBATCH, P_SIZE, 3 * members), BF16),
            pltpu.VMEM((NBATCH, 2 * members, P_SIZE), BF16),
            dma((max(nmem - 1, 1),)),
            dma((max(nmem - 1, 1),)),
            dma((max(nparts - 1, 1),)),
            dma((max(nparts - 1, 1),)),
            dma((max(nparts - 1, 1),)),
            dma((max(nparts - 1, 1),)),
            dma((max(total - 1, 1),)),
            dma((max(total - 1, 1),)),
        ],
        compiler_params=pltpu.CompilerParams(
            collective_id=0, has_side_effects=True, vmem_limit_bytes=56 * 1024 * 1024
        ),
    )(
        ensemble, partners.T, station_cells.T, owners[None], interp_weights.T,
        station_order[None], obs_values[None], obs_var[None],
    )


def solution(mesh):
    nsub, nmem = mesh.shape["sub"], mesh.shape["mem"]
    nparts = mesh.shape["dom"] * nsub

    def local(*arrays):
        nred = min(nparts, arrays[2].shape[0] // LANES)
        return body((nparts, nsub, nmem, nred), *arrays)

    return jax.shard_map(
        local,
        mesh=mesh,
        in_specs=(
            P("mem", ("groups", "dom", "sub")),
            P("groups", None),
            P("groups"),
            P("groups", None),
            P("groups"),
            P("groups"),
            P("groups"),
            P(("groups", "dom", "sub"), None),
        ),
        out_specs=P("mem", ("groups", "dom", "sub")),
        check_vma=False,
    )
```
